32 devices in a mesh: ga: 2 (over x), gy: 8 (over z, y), gx: 2 (over core).
Axes of the slice: x: 2, y: 2, z: 4, core: 2. Of those that a mesh axis runs over, the one named last changes fastest.
Arguments:
- inputs: bfloat16 [2, 32, 8192], P(None, 'ga'), parts along dimension 1, may hold values from -6 to 6
- norm_gain: bfloat16 [8192], replicated, may hold values from 0.099609375 to 1.8984375
- w_query: bfloat16 [8192, 8192], P('gx', 'gy'), may hold values from -0.0625 to 0.0625
- w_key: bfloat16 [8192, 1024], P('gx', 'gy'), may hold values from -0.0625 to 0.0625
- w_value: bfloat16 [8192, 1024], P('gx', 'gy'), may hold values from -0.0625 to 0.0625
- output_weight: bfloat16 [8192, 8192], P('gx', 'gy'), may hold values from -1.5 to 1.5
- cache_keys: bfloat16 [32, 4096, 1024], P('ga', 'gy', 'gx'), parts along dimension 0, may hold values from -810 to 810
- cache_values: bfloat16 [32, 4096, 1024], P('ga', 'gy', 'gx'), parts along dimension 0, may hold values from -6 to 6
- lengths: int32 [32], P('ga'), parts along dimension 0, may hold values from 1024 to 4096, as said below
Outputs:
- mixed: bfloat16 [2, 32, 8192], P(None, 'ga', ('gy', 'gx')), parts along dimension 1
- fresh_kv: bfloat16 [2, 32, 2, 1024], P(None, 'ga', None, 'gx'), parts along dimension 1
The draws below stay inside these ranges and needn't reach their ends.
There are 2 independent parts, one for each index of `ga`. The reference program is written for one: setup_inputs(seed, part) draws one part's arguments, and reference() takes and returns one part's arrays. A program takes and returns all parts, laid end to end along the dimension named above; an argument that names none is the same for every part. Nothing has to cross between parts.
Inputs may be any that keep to these rules, and one draw needn't show every extreme that they name: Row b's cache holds valid entries at positions below lengths[b]; some row of every group fills all 4096 positions.
All inputs are finite; a program needn't handle non-finite values.
Results may differ from the reference program's by a relative error of at most 0.012.
The reference program's roundings to bfloat16 on the way count: a program that leaves them out, or rounds other values in their place, can miss the bound.
Values may be sent and summed in bfloat16 or wider, within the bound.
A program may use at most 128 MiB of HBM per device.

```python
import math
import jax
import jax.numpy as jnp
from jax import lax

D = 8192
HQ = 64
KV = 8
HD = 128
B = 16
CACHE = 4096
STEPS = 2
QD = 8192
KVD = 1024


def draw_cache_keys(key, part):
    key = jax.random.fold_in(key, 5)
    key_base = jax.random.fold_in(key, 0)
    base = jnp.clip(jax.random.normal(key_base, (B, CACHE, KVD), jnp.float32), -6.0, 6.0)
    return base.astype(jnp.bfloat16)


def draw_lengths(key, part):
    key = jax.random.fold_in(key, 11)
    key_rows, key_full = jax.random.split(key)
    filled = jax.random.randint(key_rows, (B,), CACHE // 4, CACHE + 1, dtype=jnp.int32)
    full_row = jax.random.randint(key_full, (), 0, B, dtype=jnp.int32)
    return filled.at[full_row].set(CACHE)


def block_levels(rng, shape, cuts, least, top_value):
    factor_of, own = 1.0, jax.random.fold_in(rng, 6)
    for position, shards_of in cuts:
        heights = jnp.exp(jax.random.uniform(jax.random.fold_in(own, position), (shards_of,), jnp.float32, least / len(cuts), top_value / len(cuts)))
        factor_of = factor_of * jnp.repeat(heights, shape[position] // shards_of).reshape([-1 if axis == position else 1 for axis in range(len(shape))])
    return factor_of


def centred(stream_key, dims, spread, reach, pieces=(), kind=jnp.bfloat16):
    values = spread * jax.random.normal(stream_key, dims, jnp.float32)
    if pieces:
        values = values * block_levels(stream_key, dims, pieces, -0.22, 0.18)
    return jnp.clip(values, -reach, reach).astype(kind)


def setup_inputs(seed: int = 0, part: int = 0) -> dict:
    splits = jax.random.split(jax.random.key(seed), 10)
    part_keys = jax.random.split(jax.random.fold_in(splits[9], part), 10)
    inputs = centred(part_keys[0], (STEPS, B, D), 1.0, 6.0)
    norm_gain = jnp.clip(1.0 + 0.18 * jax.random.normal(splits[1], (D,), jnp.float32), 0.099609375, 1.8984375).astype(jnp.bfloat16)
    w_query = centred(splits[2], (D, QD), D ** -0.5, 0.0625, ((0, 2), (1, 8)))
    w_key = centred(splits[3], (D, KVD), D ** -0.5, 0.0625, ((0, 2), (1, 8)))
    w_value = centred(splits[4], (D, KVD), D ** -0.5, 0.0625, ((0, 2), (1, 8)))
    output_weight = centred(splits[5], (QD, D), 16 ** -0.5, 1.5, ((0, 2), (1, 8)))
    cache_keys = draw_cache_keys(jax.random.fold_in(jax.random.fold_in(splits[9], part), 71), part)
    cache_values = centred(part_keys[7], (B, CACHE, KVD), 1.0, 6.0, ((1, 8), (2, 2)))
    lengths = draw_lengths(jax.random.fold_in(jax.random.fold_in(splits[9], part), 71), part)
    return dict(inputs=inputs, norm_gain=norm_gain, w_query=w_query, w_key=w_key, w_value=w_value, output_weight=output_weight, cache_keys=cache_keys, cache_values=cache_values, lengths=lengths)


THETA = 500000.0
EPS = 1e-05

def rotate(values, positions):
    half_width = values.shape[-1] // 2
    frequency = jnp.exp(jnp.arange(half_width, dtype=jnp.float32) * (-2.0 * math.log(THETA) / values.shape[-1]))
    angles = positions[..., None, None] * frequency
    cos_part = jnp.cos(angles)
    sine_part = jnp.sin(angles)
    first_half = values[..., :half_width]
    second_half = values[..., half_width:]
    return jnp.concatenate([first_half * cos_part - second_half * sine_part, second_half * cos_part + first_half * sine_part], axis=-1)

def reference(inputs, norm_gain, w_query, w_key, w_value, output_weight, cache_keys, cache_values, lengths):
    group_size = HQ // KV
    score_scale = HD ** (-0.5)
    keys_cache = cache_keys.astype(jnp.float32).reshape(B, CACHE, KV, HD)
    values_cache = cache_values.astype(jnp.float32).reshape(B, CACHE, KV, HD)
    valid_mask = jnp.arange(CACHE, dtype=jnp.int32)[None, :] < lengths[:, None]
    fresh_keys = []
    fresh_values = []
    mixed_list = []
    fresh_list = []
    for step_index in range(STEPS):
        states = inputs[step_index].astype(jnp.float32)
        normalized_input = (states * lax.rsqrt(lax.optimization_barrier(jnp.mean(states * states, axis=-1, keepdims=True)) + EPS) * norm_gain.astype(jnp.float32)).astype(jnp.bfloat16)
        q_full = jnp.dot(normalized_input, w_query, preferred_element_type=jnp.float32)
        k_full = jnp.dot(normalized_input, w_key, preferred_element_type=jnp.float32)
        v_full = jnp.dot(normalized_input, w_value, preferred_element_type=jnp.float32)
        positions = lengths.astype(jnp.float32) + step_index
        queries = rotate(q_full.reshape(B, HQ, HD), positions).astype(jnp.bfloat16)
        queries = lax.optimization_barrier(queries).astype(jnp.float32).reshape(B, KV, group_size, HD)
        keys_raw = lax.optimization_barrier(k_full.astype(jnp.bfloat16)).astype(jnp.float32)
        keys_new = rotate(keys_raw.reshape(B, KV, HD), positions).astype(jnp.bfloat16)
        values_new = v_full.astype(jnp.bfloat16)
        fresh_keys.append(keys_new)
        fresh_values.append(values_new.reshape(B, KV, HD))
        fresh_list.append(jnp.stack([keys_new.reshape(B, KV * HD), values_new], axis=1))
        keys_seen = jnp.stack(fresh_keys, axis=1).astype(jnp.float32)
        values_seen = jnp.stack(fresh_values, axis=1).astype(jnp.float32)
        cache_score = jnp.einsum('bkgd,bpkd->bkgp', queries, keys_cache) * score_scale
        cache_score = jnp.where(valid_mask[:, None, None, :], cache_score, -jnp.inf)
        fresh_score = jnp.einsum('bkgd,bjkd->bkgj', queries, keys_seen) * score_scale
        peak_score = jnp.maximum(lax.optimization_barrier(jnp.max(cache_score, axis=-1)), lax.optimization_barrier(jnp.max(fresh_score, axis=-1)))
        cache_weight = jnp.exp(cache_score - peak_score[..., None])
        fresh_weight = jnp.exp(fresh_score - peak_score[..., None])
        total = lax.optimization_barrier(jnp.sum(cache_weight, axis=-1)) + lax.optimization_barrier(jnp.sum(fresh_weight, axis=-1))
        rounded_cache = lax.optimization_barrier(cache_weight.astype(jnp.bfloat16)).astype(jnp.float32)
        rounded_fresh = lax.optimization_barrier(fresh_weight.astype(jnp.bfloat16)).astype(jnp.float32)
        acc = jnp.einsum('bkgp,bpkd->bkgd', rounded_cache, values_cache) + jnp.einsum('bkgj,bjkd->bkgd', rounded_fresh, values_seen)
        attention_result = (acc / total[..., None]).astype(jnp.bfloat16).reshape(B, HQ * HD)
        projected = jnp.dot(attention_result, output_weight, preferred_element_type=jnp.float32)
        mixed_list.append((states + projected).astype(jnp.bfloat16))
    return (jnp.stack(mixed_list, axis=0), jnp.stack(fresh_list, axis=0))
```

```python
import math

import jax
import jax.numpy as jnp
from jax import lax
from jax.sharding import PartitionSpec as P

HQ = 64
KV = 8
HD = 128


THETA = 500000.0
EPS = 1e-05


def rotate(values, positions):
    half_width = values.shape[-1] // 2
    frequency = jnp.exp(
        jnp.arange(half_width, dtype=jnp.float32) * (-2.0 * math.log(THETA) / values.shape[-1])
    )
    angles = positions[..., None, None] * frequency
    cos_part = jnp.cos(angles)
    sine_part = jnp.sin(angles)
    first_half = values[..., :half_width]
    second_half = values[..., half_width:]
    return jnp.concatenate(
        [
            first_half * cos_part - second_half * sine_part,
            second_half * cos_part + first_half * sine_part,
        ],
        axis=-1,
    )


def on_device_plain(
    inputs, norm_gain, w_query, w_key, w_value, output_weight, cache_keys, cache_values, lengths
):
    n_gx = lax.axis_size("gx")
    gx_pos = lax.axis_index("gx")
    gy_pos = lax.axis_index("gy")
    steps_total = inputs.shape[0]
    batch_rows = inputs.shape[1]
    input_half_width = w_query.shape[0]
    cache_span = cache_keys.shape[1]
    kv_local = cache_keys.shape[2]
    heads_kv = kv_local // HD
    group_size = HQ // KV
    heads_here = heads_kv * group_size
    q_width = heads_here * HD
    output_columns = output_weight.shape[1]
    own_cols = output_columns // n_gx
    score_scale = HD ** (-0.5)
    states = inputs.astype(jnp.float32)
    normalized_input = (
        states
        * lax.rsqrt(jnp.mean(states * states, axis=-1, keepdims=True) + EPS)
        * norm_gain.astype(jnp.float32)
    ).astype(jnp.bfloat16)
    block = lax.dynamic_slice_in_dim(
        normalized_input, gx_pos * input_half_width, input_half_width, 2
    )
    residual_cols = lax.dynamic_slice_in_dim(
        states, gy_pos * output_columns + gx_pos * own_cols, own_cols, 2
    )
    offsets = gy_pos * cache_span + jnp.arange(cache_span, dtype=jnp.int32)
    valid_mask = offsets[None, :] < lengths[:, None]
    keys_here = cache_keys.reshape(batch_rows, cache_span, heads_kv, HD)
    values_here = cache_values.reshape(batch_rows, cache_span, heads_kv, HD)
    q_part = jnp.einsum("cbd,de->cbe", block, w_query, preferred_element_type=jnp.float32)
    k_part = jnp.einsum("cbd,de->cbe", block, w_key, preferred_element_type=jnp.float32)
    v_part = jnp.einsum("cbd,de->cbe", block, w_value, preferred_element_type=jnp.float32)
    q_sum, k_sum, v_sum = lax.psum((q_part, k_part, v_part), "gx")
    positions = (
        lengths.astype(jnp.float32)[None, :]
        + jnp.arange(steps_total, dtype=jnp.float32)[:, None]
    )
    gather = lambda a: lax.all_gather(a, "gy", axis=2, tiled=True)
    mine = lambda a, width: lax.dynamic_slice_in_dim(a, gx_pos * width, width, 2)
    q_all = gather(
        q_sum.astype(jnp.float32)
        if q_sum.shape[2] % HD
        else rotate(q_sum.reshape(steps_total, batch_rows, -1, HD), positions)
        .astype(jnp.bfloat16)
        .reshape(q_sum.shape)
    )
    queries = mine(q_all, q_width).reshape(steps_total, batch_rows, heads_kv, group_size, HD)
    if q_sum.shape[2] % HD:
        queries = rotate(
            queries.reshape(steps_total, batch_rows, -1, HD), positions
        ).astype(jnp.bfloat16).reshape(queries.shape)
    keys_raw = mine(gather(k_sum.astype(jnp.bfloat16)), kv_local)
    values_new = mine(gather(v_sum.astype(jnp.bfloat16)), kv_local)
    keys_new = (
        rotate(keys_raw.astype(jnp.float32).reshape(steps_total, batch_rows, heads_kv, HD), positions)
        .astype(jnp.bfloat16)
        .reshape(steps_total, batch_rows, kv_local)
    )
    fresh_all = jnp.stack([keys_new, values_new], axis=2)
    cache_score = (
        jnp.einsum("cbkgd,bpkd->bkcgp", queries, keys_here, preferred_element_type=jnp.float32)
        * score_scale
    )
    cache_score = jnp.where(valid_mask[:, None, None, None, :], cache_score, -jnp.inf)
    fresh_score = (
        jnp.einsum(
            "cbkgd,jbkd->bkcgj",
            queries,
            keys_new.reshape(steps_total, batch_rows, heads_kv, HD),
            preferred_element_type=jnp.float32,
        )
        * score_scale
    )
    order = jnp.arange(steps_total, dtype=jnp.int32)
    causal = order[None, :] <= order[:, None]
    fresh_score = jnp.where(causal[:, None, :], fresh_score, -jnp.inf)
    local_peak = jnp.maximum(jnp.max(cache_score, axis=-1), jnp.max(fresh_score, axis=-1))
    peak_score = lax.pmax(local_peak, "gy")
    cache_weight = jnp.exp(cache_score - peak_score[..., None])
    fresh_weight = jnp.exp(fresh_score - peak_score[..., None])
    cache_total = jnp.sum(cache_weight, axis=-1)
    fresh_total = jnp.sum(fresh_weight, axis=-1)
    cache_acc = jnp.einsum(
        "bkcgp,bpkd->bkcgd",
        cache_weight.astype(jnp.bfloat16),
        values_here,
        preferred_element_type=jnp.float32,
    )
    fresh_acc = jnp.einsum(
        "bkcgj,jbkd->bkcgd",
        fresh_weight.astype(jnp.bfloat16),
        values_new.reshape(steps_total, batch_rows, heads_kv, HD),
        preferred_element_type=jnp.float32,
    )
    acc_sum, total_sum = lax.psum((cache_acc, cache_total), "gy")
    attention_result = ((acc_sum + fresh_acc) / (total_sum + fresh_total)[..., None]).astype(
        jnp.bfloat16
    )
    attention_result = jnp.transpose(attention_result, (2, 0, 1, 3, 4)).reshape(
        steps_total, batch_rows, q_width
    )
    output_piece = jnp.einsum(
        "yjz,zo->yjo", attention_result, output_weight, preferred_element_type=jnp.float32
    )
    projected = lax.psum_scatter(output_piece, "gx", scatter_dimension=2, tiled=True)
    mixed_all = (residual_cols + projected).astype(jnp.bfloat16)
    return (mixed_all, fresh_all)


def solution(mesh):
    return jax.shard_map(
        on_device_plain,
        mesh=mesh,
        in_specs=(
            P(None, "ga", None),
            P(),
            P("gx", "gy"),
            P("gx", "gy"),
            P("gx", "gy"),
            P("gx", "gy"),
            P("ga", "gy", "gx"),
            P("ga", "gy", "gx"),
            P("ga"),
        ),
        out_specs=(P(None, "ga", ("gy", "gx")), P(None, "ga", None, "gx")),
        check_vma=False,
    )
```

```python
import functools
import math

import jax
import jax.numpy as jnp
import numpy as np
from jax import lax
from jax.experimental import pallas as pl
from jax.experimental.pallas import tpu as pltpu
from jax.sharding import PartitionSpec as P

HQ = 64
KV = 8
HD = 128


THETA = 500000.0
EPS = 1e-05


def rotate(values, positions):
    half_width = values.shape[-1] // 2
    frequency = jnp.exp(
        jnp.arange(half_width, dtype=jnp.float32) * (-2.0 * math.log(THETA) / values.shape[-1])
    )
    angles = positions[..., None, None] * frequency
    cos_part = jnp.cos(angles)
    sine_part = jnp.sin(angles)
    first_half = values[..., :half_width]
    second_half = values[..., half_width:]
    return jnp.concatenate(
        [
            first_half * cos_part - second_half * sine_part,
            second_half * cos_part + first_half * sine_part,
        ],
        axis=-1,
    )


def on_device_plain(
    inputs, norm_gain, w_query, w_key, w_value, output_weight, cache_keys, cache_values, lengths
):
    n_gx = lax.axis_size("gx")
    gx_pos = lax.axis_index("gx")
    gy_pos = lax.axis_index("gy")
    steps_total = inputs.shape[0]
    batch_rows = inputs.shape[1]
    input_half_width = w_query.shape[0]
    cache_span = cache_keys.shape[1]
    kv_local = cache_keys.shape[2]
    heads_kv = kv_local // HD
    group_size = HQ // KV
    heads_here = heads_kv * group_size
    q_width = heads_here * HD
    output_columns = output_weight.shape[1]
    own_cols = output_columns // n_gx
    score_scale = HD ** (-0.5)
    states = inputs.astype(jnp.float32)
    normalized_input = (
        states
        * lax.rsqrt(jnp.mean(states * states, axis=-1, keepdims=True) + EPS)
        * norm_gain.astype(jnp.float32)
    ).astype(jnp.bfloat16)
    block = lax.dynamic_slice_in_dim(
        normalized_input, gx_pos * input_half_width, input_half_width, 2
    )
    residual_cols = lax.dynamic_slice_in_dim(
        states, gy_pos * output_columns + gx_pos * own_cols, own_cols, 2
    )
    offsets = gy_pos * cache_span + jnp.arange(cache_span, dtype=jnp.int32)
    valid_mask = offsets[None, :] < lengths[:, None]
    keys_here = cache_keys.reshape(batch_rows, cache_span, heads_kv, HD)
    values_here = cache_values.reshape(batch_rows, cache_span, heads_kv, HD)
    q_part = jnp.einsum("cbd,de->cbe", block, w_query, preferred_element_type=jnp.float32)
    k_part = jnp.einsum("cbd,de->cbe", block, w_key, preferred_element_type=jnp.float32)
    v_part = jnp.einsum("cbd,de->cbe", block, w_value, preferred_element_type=jnp.float32)
    q_sum, k_sum, v_sum = lax.psum((q_part, k_part, v_part), "gx")
    positions = (
        lengths.astype(jnp.float32)[None, :]
        + jnp.arange(steps_total, dtype=jnp.float32)[:, None]
    )
    gather = lambda a: lax.all_gather(a, "gy", axis=2, tiled=True)
    mine = lambda a, width: lax.dynamic_slice_in_dim(a, gx_pos * width, width, 2)
    q_all = gather(
        q_sum.astype(jnp.float32)
        if q_sum.shape[2] % HD
        else rotate(q_sum.reshape(steps_total, batch_rows, -1, HD), positions)
        .astype(jnp.bfloat16)
        .reshape(q_sum.shape)
    )
    queries = mine(q_all, q_width).reshape(steps_total, batch_rows, heads_kv, group_size, HD)
    if q_sum.shape[2] % HD:
        queries = rotate(
            queries.reshape(steps_total, batch_rows, -1, HD), positions
        ).astype(jnp.bfloat16).reshape(queries.shape)
    keys_raw = mine(gather(k_sum.astype(jnp.bfloat16)), kv_local)
    values_new = mine(gather(v_sum.astype(jnp.bfloat16)), kv_local)
    keys_new = (
        rotate(keys_raw.astype(jnp.float32).reshape(steps_total, batch_rows, heads_kv, HD), positions)
        .astype(jnp.bfloat16)
        .reshape(steps_total, batch_rows, kv_local)
    )
    fresh_all = jnp.stack([keys_new, values_new], axis=2)
    cache_score = (
        jnp.einsum("cbkgd,bpkd->bkcgp", queries, keys_here, preferred_element_type=jnp.float32)
        * score_scale
    )
    cache_score = jnp.where(valid_mask[:, None, None, None, :], cache_score, -jnp.inf)
    fresh_score = (
        jnp.einsum(
            "cbkgd,jbkd->bkcgj",
            queries,
            keys_new.reshape(steps_total, batch_rows, heads_kv, HD),
            preferred_element_type=jnp.float32,
        )
        * score_scale
    )
    order = jnp.arange(steps_total, dtype=jnp.int32)
    causal = order[None, :] <= order[:, None]
    fresh_score = jnp.where(causal[:, None, :], fresh_score, -jnp.inf)
    local_peak = jnp.maximum(jnp.max(cache_score, axis=-1), jnp.max(fresh_score, axis=-1))
    peak_score = lax.pmax(local_peak, "gy")
    cache_weight = jnp.exp(cache_score - peak_score[..., None])
    fresh_weight = jnp.exp(fresh_score - peak_score[..., None])
    cache_total = jnp.sum(cache_weight, axis=-1)
    fresh_total = jnp.sum(fresh_weight, axis=-1)
    cache_acc = jnp.einsum(
        "bkcgp,bpkd->bkcgd",
        cache_weight.astype(jnp.bfloat16),
        values_here,
        preferred_element_type=jnp.float32,
    )
    fresh_acc = jnp.einsum(
        "bkcgj,jbkd->bkcgd",
        fresh_weight.astype(jnp.bfloat16),
        values_new.reshape(steps_total, batch_rows, heads_kv, HD),
        preferred_element_type=jnp.float32,
    )
    acc_sum, total_sum = lax.psum((cache_acc, cache_total), "gy")
    attention_result = ((acc_sum + fresh_acc) / (total_sum + fresh_total)[..., None]).astype(
        jnp.bfloat16
    )
    attention_result = jnp.transpose(attention_result, (2, 0, 1, 3, 4)).reshape(
        steps_total, batch_rows, q_width
    )
    output_piece = jnp.einsum(
        "yjz,zo->yjo", attention_result, output_weight, preferred_element_type=jnp.float32
    )
    projected = lax.psum_scatter(output_piece, "gx", scatter_dimension=2, tiled=True)
    mixed_all = (residual_cols + projected).astype(jnp.bfloat16)
    return (mixed_all, fresh_all)


MESH = pl.DeviceIdType.MESH
LOW = -1e30
CHUNKS = 8


def block_kernel(
    n_gy,
    len_ref, gain_ref, freq_ref, x_hbm, wq_hbm, wk_hbm, wv_hbm, wo_hbm, kc_hbm, vc_hbm,
    mixed_ref, fresh_ref,
    x_v, xn_v, w_v, wo_v, kc_v, vc_v, part, part_in, qsort, pack, gath, kvf,
    acc_s, acc_r, ml_s, ml_r, fresh_acc, att, flat, lhs, po_s, po_r,
    sem_x, sem_wq, sem_wk, sem_wv, sem_kc, sem_vc, sem_wo,
    pair_s, pair_r, gath_s, gath_r, accs, accr, mls, mlr, atts, attr, out_s, out_r,
):
    gx = lax.axis_index("gx")
    gy = lax.axis_index("gy")
    half = w_v.shape[0]
    qw = wq_hbm.shape[1]
    heads = kc_hbm.shape[2] // HD
    rows = kc_hbm.shape[0]
    span = kc_hbm.shape[1]
    own = rows // n_gy
    group = HQ // KV
    hb = rows // 2
    combos = own * heads
    per_gx = n_gy // 2
    target = gy // per_gx
    scale = HD ** (-0.5)
    step_rows = half // CHUNKS

    def owner_of(d):
        return lax.rem(gy + 1 + d, n_gy)

    copy_x = pltpu.make_async_copy(x_hbm, x_v, sem_x)
    copy_x.start()

    def wq_copies(c):
        r = pl.ds(c * step_rows, step_rows)
        return (
            pltpu.make_async_copy(wq_hbm.at[r], w_v.at[r, pl.ds(0, qw)], sem_wq.at[c]),
            pltpu.make_async_copy(wk_hbm.at[r], w_v.at[r, pl.ds(qw, HD)], sem_wk.at[c]),
            pltpu.make_async_copy(wv_hbm.at[r], w_v.at[r, pl.ds(qw + HD, HD)], sem_wv.at[c]),
        )

    def cache_copies(d):
        r = pl.ds(owner_of(d) * own, own)
        return (
            pltpu.make_async_copy(kc_hbm.at[r], kc_v.at[d], sem_kc.at[d]),
            pltpu.make_async_copy(vc_hbm.at[r], vc_v.at[d], sem_vc.at[d]),
        )

    oc = wo_hbm.shape[1] // 2
    ok = half // 4

    def wo_copy(p, c):
        which = (1 - gx) if p == 0 else gx
        r = pl.ds(c * ok, ok)
        return pltpu.make_async_copy(
            wo_hbm.at[r, pl.ds(pl.multiple_of(which * oc, oc), oc)], wo_v.at[p, r], sem_wo.at[p * 4 + c]
        )

    for c in range(CHUNKS):
        for copy in wq_copies(c):
            copy.start()

    barrier = pltpu.get_barrier_semaphore()
    for d in range(1, n_gy):
        for g in range(2):
            pl.semaphore_signal(
                barrier, inc=1, device_id={"gy": lax.rem(gy + d, n_gy), "gx": g}, device_id_type=MESH
            )
    pl.semaphore_signal(barrier, inc=1, device_id={"gx": 1 - gx}, device_id_type=MESH)

    for d in range(n_gy):
        for copy in cache_copies(d):
            copy.start()
    for p in range(2):
        for c in range(4):
            wo_copy(p, c).start()

    row16 = lax.broadcasted_iota(jnp.int32, (2 * hb, HD), 0)
    lane16 = lax.broadcasted_iota(jnp.int32, (2 * hb, HD), 1)
    pos = jnp.zeros((2 * hb, HD), jnp.float32)
    for r in range(hb):
        pos = jnp.where(row16 % hb == r, len_ref[gx * hb + r].astype(jnp.float32), pos)
    pos = pos + (row16 // hb).astype(jnp.float32)
    angle = pos * freq_ref[...]
    cos_t = jnp.cos(angle)
    sin_t = jnp.sin(angle)
    sin_t = jnp.where(lane16 < HD // 2, -sin_t, sin_t)

    def rope(u):
        return u * cos_t + pltpu.roll(u, HD // 2, 1) * sin_t

    copy_x.wait()
    width = x_v.shape[1]
    total = jnp.zeros((x_v.shape[0], 1024), jnp.float32)
    for c in range(width // 1024):
        xf = x_v[:, c * 1024 : (c + 1) * 1024].astype(jnp.float32)
        total = total + xf * xf
    inv = lax.rsqrt(jnp.sum(total, axis=1, keepdims=True) * (1.0 / width) + EPS)
    for c in range(half // 1024):
        cols = pl.ds(pl.multiple_of(gx * half + c * 1024, 1024), 1024)
        xf = x_v[:, cols].astype(jnp.float32)
        xn_v[:, c * 1024 : (c + 1) * 1024] = (xf * inv * gain_ref[:, cols]).astype(jnp.bfloat16)

    acc = jnp.zeros((x_v.shape[0], w_v.shape[1]), jnp.float32)
    for c in range(CHUNKS):
        for copy in wq_copies(c):
            copy.wait()
        r = slice(c * step_rows, (c + 1) * step_rows)
        acc = acc + jnp.dot(xn_v[:, r], w_v[r, :], preferred_element_type=jnp.float32)
    for c in range(2):
        for s in range(2):
            part[c, s * hb : (s + 1) * hb, :] = acc[s * rows + c * hb : s * rows + (c + 1) * hb]

    pl.semaphore_wait(barrier, 2 * n_gy - 1)
    pair = pltpu.make_async_remote_copy(
        src_ref=part.at[1 - gx], dst_ref=part_in, send_sem=pair_s, recv_sem=pair_r,
        device_id={"gx": 1 - gx}, device_id_type=MESH,
    )
    pair.start()
    pair.wait_recv()
    tot = part[gx] + part_in[...]
    for g in range(group):
        u = rope(tot[:, g * HD : (g + 1) * HD])
        for s in range(2):
            qsort[pl.ds(s * group + g, hb, stride=2 * group), :] = u[s * hb : (s + 1) * hb]
    nq = hb * 2 * group
    pack[0:nq, :] = qsort[...].astype(jnp.bfloat16)
    kraw = tot[:, qw : qw + HD].astype(jnp.bfloat16).astype(jnp.float32)
    pack[nq : nq + 2 * hb, :] = rope(kraw).astype(jnp.bfloat16)
    pack[nq + 2 * hb : nq + 4 * hb, :] = tot[:, qw + HD : qw + 2 * HD].astype(jnp.bfloat16)

    slot = lax.rem(gy, per_gx) * 2 + gx
    here = target == gx

    def gather_copy(i, at):
        return pltpu.make_async_remote_copy(
            src_ref=pack, dst_ref=gath.at[at], send_sem=gath_s.at[i], recv_sem=gath_r.at[at],
            device_id={"gy": lax.rem(gy + i, n_gy), "gx": target}, device_id_type=MESH,
        )

    for i in range(1, n_gy):
        gather_copy(i, slot).start()

    @pl.when(here)
    def _():
        gath[slot] = pack[...]

    @pl.when(jnp.logical_not(here))
    def _():
        gather_copy(0, slot).start()

    for k in range(2 * per_gx):
        mine = jnp.logical_and(here, slot == k)

        @pl.when(jnp.logical_not(mine))
        def _():
            gather_copy(1, k).wait_recv()

    lane_ml = lax.broadcasted_iota(jnp.int32, (2 * group, HD), 1)
    lane_s = lax.broadcasted_iota(jnp.int32, (2 * group, span), 1) + gy * span

    def send_acc(d):
        return pltpu.make_async_remote_copy(
            src_ref=acc_s.at[d], dst_ref=acc_r.at[d], send_sem=accs.at[d], recv_sem=accr.at[d],
            device_id={"gy": owner_of(d)}, device_id_type=MESH,
        )

    def send_ml(d):
        return pltpu.make_async_remote_copy(
            src_ref=ml_s.at[d], dst_ref=ml_r.at[d], send_sem=mls.at[d], recv_sem=mlr.at[d],
            device_id={"gy": owner_of(d)}, device_id_type=MESH,
        )

    nqr = 2 * group

    def attend(d, carry):
        for copy in cache_copies(d):
            copy.wait()
        owner = owner_of(d)
        ml = jnp.zeros((nqr, HD), jnp.float32)
        for i in range(own):
            b = owner * own + i
            c = b // hb
            bl = lax.rem(b, hb)
            seen = lane_s < len_ref[b]
            for h in range(heads):
                k = i * heads + h
                q = gath[h * 2 + c, pl.ds(pl.multiple_of(bl * nqr, nqr), nqr), :]
                score = lax.dot_general(
                    q, kc_v[d, i, :, h * HD : (h + 1) * HD], (((1,), (1,)), ((), ())),
                    preferred_element_type=jnp.float32,
                ) * scale
                score = jnp.where(seen, score, LOW)
                m = jnp.max(score, axis=1, keepdims=True)
                p = jnp.where(seen, jnp.exp(score - m), 0.0)
                o = jnp.dot(
                    p.astype(jnp.bfloat16), vc_v[d, i, :, h * HD : (h + 1) * HD],
                    preferred_element_type=jnp.float32,
                )
                acc_s[d, k * nqr : (k + 1) * nqr, :] = o.astype(jnp.bfloat16)
                ml = jnp.where(lane_ml == k, m, ml)
                ml = jnp.where(lane_ml == k + HD // 2, jnp.sum(p, axis=1, keepdims=True), ml)
        ml_s[d] = ml

        @pl.when(d < n_gy - 1)
        def _():
            send_acc(d).start()
            send_ml(d).start()

        return carry

    lax.fori_loop(0, n_gy, attend, 0)

    for k in range(2 * heads):
        kvf[k] = gath[k, nq : nq + 4 * hb, :].astype(jnp.float32)
    for s in range(2):
        for t in range(2):
            for h in range(heads):
                at = t * 2 * hb + s * hb
                fresh_ref[s * rows : (s + 1) * rows, (t * heads + h) * HD : (t * heads + h + 1) * HD] = (
                    jnp.concatenate([kvf[2 * h, at : at + hb, :], kvf[2 * h + 1, at : at + hb, :]], axis=0)
                ).astype(jnp.bfloat16)

    later = lax.broadcasted_iota(jnp.int32, (nqr, 1), 0) >= group
    mlf = jnp.zeros((nqr, HD), jnp.float32)
    for i in range(own):
        b = gy * own + i
        c = b // hb
        bl = lax.rem(b, hb)
        for h in range(heads):
            k = i * heads + h
            q = gath[h * 2 + c, pl.ds(pl.multiple_of(bl * nqr, nqr), nqr), :].astype(jnp.float32)
            f = []
            for s in range(2):
                key = kvf[h * 2 + c, pl.ds(s * hb + bl, 1), :]
                f.append(jnp.sum(q * key, axis=1, keepdims=True) * scale)
            f[1] = jnp.where(later, f[1], LOW)
            m = jnp.maximum(f[0], f[1])
            p0 = jnp.exp(f[0] - m)
            p1 = jnp.where(later, jnp.exp(f[1] - m), 0.0)
            v0 = kvf[h * 2 + c, pl.ds(2 * hb + bl, 1), :]
            v1 = kvf[h * 2 + c, pl.ds(3 * hb + bl, 1), :]
            fresh_acc[k * nqr : (k + 1) * nqr, :] = (
                p0.astype(jnp.bfloat16).astype(jnp.float32) * v0
                + p1.astype(jnp.bfloat16).astype(jnp.float32) * v1
            )
            mlf = jnp.where(lane_ml == k, m, mlf)
            mlf = jnp.where(lane_ml == k + HD // 2, p0 + p1, mlf)

    for d in range(n_gy - 1):
        send_ml(d).wait_recv()
    ml_all = [ml_r[d] for d in range(n_gy - 1)] + [ml_s[n_gy - 1], mlf]
    peak = ml_all[0]
    for ml in ml_all[1:]:
        peak = jnp.maximum(peak, ml)
    factors = [jnp.exp(ml - peak) for ml in ml_all]
    weight = jnp.zeros_like(peak)
    for f, ml in zip(factors, ml_all):
        weight = weight + f * pltpu.roll(ml, HD // 2, 1)
    for d in range(n_gy - 1):
        send_acc(d).wait_recv()
    for k in range(combos):
        r = slice(k * nqr, (k + 1) * nqr)
        o = factors[n_gy][:, k : k + 1] * fresh_acc[r, :]
        for d in range(n_gy):
            a = acc_r[d, r, :] if d < n_gy - 1 else acc_s[d, r, :]
            o = o + factors[d][:, k : k + 1] * a.astype(jnp.float32)
        att[gy, r, :] = (o / weight[:, k : k + 1]).astype(jnp.bfloat16)

    def att_copy(d, at):
        return pltpu.make_async_remote_copy(
            src_ref=att.at[at], dst_ref=att.at[at], send_sem=atts.at[d - 1], recv_sem=attr.at[at],
            device_id={"gy": lax.rem(gy + d, n_gy)}, device_id_type=MESH,
        )

    for d in range(1, n_gy):
        att_copy(d, gy).start()
    for d in range(1, n_gy):
        att_copy(d, lax.rem(gy + d, n_gy)).wait_recv()
    size = combos * nqr
    for j in range(n_gy):
        flat[j * size : (j + 1) * size, :] = att[j].astype(jnp.float32)
    for h in range(heads):
        for g in range(group):
            for s in range(2):
                lhs[s * rows : (s + 1) * rows, (h * group + g) * HD : (h * group + g + 1) * HD] = flat[
                    pl.ds(h * nqr + s * group + g, rows, stride=heads * nqr), :
                ].astype(jnp.bfloat16)

    def project(p):
        total = jnp.zeros((2 * rows, oc), jnp.float32)
        for c in range(4):
            wo_copy(p, c).wait()
            r = slice(c * ok, (c + 1) * ok)
            total = total + jnp.dot(lhs[:, r], wo_v[p, r, :], preferred_element_type=jnp.float32)
        return total

    po_s[...] = project(0)
    out_copy = pltpu.make_async_remote_copy(
        src_ref=po_s, dst_ref=po_r, send_sem=out_s, recv_sem=out_r,
        device_id={"gx": 1 - gx}, device_id_type=MESH,
    )
    out_copy.start()
    mine_out = project(1)
    residual = x_v[:, pl.ds(pl.multiple_of((gy * 2 + gx) * oc, oc), oc)].astype(jnp.float32)
    out_copy.wait_recv()
    mixed_ref[...] = (residual + (mine_out + po_r[...])).astype(jnp.bfloat16)

    pair.wait_send()
    for i in range(1, n_gy):
        gather_copy(i, slot).wait_send()

    @pl.when(jnp.logical_not(here))
    def _():
        gather_copy(0, slot).wait_send()

    for d in range(n_gy - 1):
        send_acc(d).wait_send()
        send_ml(d).wait_send()
    for d in range(1, n_gy):
        att_copy(d, gy).wait_send()
    out_copy.wait_send()


def on_device_kernel(
    inputs, norm_gain, w_query, w_key, w_value, output_weight, cache_keys, cache_values, lengths
):
    n_gy = lax.axis_size("gy")
    steps, rows, width = inputs.shape
    half, qw = w_query.shape
    span, kvl = cache_keys.shape[1:]
    heads = kvl // HD
    own = rows // n_gy
    group = HQ // KV
    nqr = 2 * group
    hb = rows // 2
    size = own * heads * nqr
    oc = output_weight.shape[1] // 2
    npack = hb * nqr + 4 * hb
    freq = np.exp(np.arange(HD // 2) * (-2.0 * math.log(THETA) / HD))
    freq = jnp.asarray(np.tile(freq, 2)[None, :], jnp.float32)
    f32, b16 = jnp.float32, jnp.bfloat16
    dma = pltpu.SemaphoreType.DMA
    vmem = pl.BlockSpec(memory_space=pltpu.VMEM)
    hbm = pl.BlockSpec(memory_space=pl.ANY)
    mixed, fresh = pl.pallas_call(
        functools.partial(block_kernel, n_gy),
        out_shape=(
            jax.ShapeDtypeStruct((steps * rows, oc), b16),
            jax.ShapeDtypeStruct((steps * rows, 2 * kvl), b16),
        ),
        in_specs=[pl.BlockSpec(memory_space=pltpu.SMEM), vmem, vmem] + [hbm] * 7,
        out_specs=(vmem, vmem),
        scratch_shapes=[
            pltpu.VMEM((steps * rows, width), b16),
            pltpu.VMEM((steps * rows, half), b16),
            pltpu.VMEM((half, qw + 2 * HD), b16),
            pltpu.VMEM((2, half, oc), b16),
            pltpu.VMEM((n_gy, own, span, kvl), b16),
            pltpu.VMEM((n_gy, own, span, kvl), b16),
            pltpu.VMEM((2, steps * hb, qw + 2 * HD), f32),
            pltpu.VMEM((steps * hb, qw + 2 * HD), f32),
            pltpu.VMEM((hb * nqr, HD), f32),
            pltpu.VMEM((npack, HD), b16),
            pltpu.VMEM((2 * heads, npack, HD), b16),
            pltpu.VMEM((2 * heads, 4 * hb, HD), f32),
            pltpu.VMEM((n_gy, size, HD), b16),
            pltpu.VMEM((n_gy - 1, size, HD), b16),
            pltpu.VMEM((n_gy, nqr, HD), f32),
            pltpu.VMEM((n_gy - 1, nqr, HD), f32),
            pltpu.VMEM((size, HD), f32),
            pltpu.VMEM((n_gy, size, HD), b16),
            pltpu.VMEM((n_gy * size, HD), f32),
            pltpu.VMEM((steps * rows, half), b16),
            pltpu.VMEM((steps * rows, oc), f32),
            pltpu.VMEM((steps * rows, oc), f32),
            dma, dma((CHUNKS,)), dma((CHUNKS,)), dma((CHUNKS,)), dma((n_gy,)), dma((n_gy,)), dma((8,)),
            dma, dma, dma((n_gy,)), dma((2 * heads,)),
            dma((n_gy - 1,)), dma((n_gy - 1,)), dma((n_gy - 1,)), dma((n_gy - 1,)),
            dma((n_gy - 1,)), dma((n_gy,)), dma, dma,
        ],
        compiler_params=pltpu.CompilerParams(
            collective_id=0, has_side_effects=True, vmem_limit_bytes=52 * 1024 * 1024
        ),
        name="decode_block",
    )(
        lengths, norm_gain.astype(f32).reshape(1, width), freq, inputs.reshape(steps * rows, width),
        w_query, w_key, w_value, output_weight, cache_keys, cache_values,
    )
    return mixed.reshape(steps, rows, oc), fresh.reshape(steps, rows, 2, kvl)


def on_device(*args):
    inputs, _, w_query, w_key, _, output_weight, cache_keys, _, _ = args
    n_gy, n_gx = lax.axis_size("gy"), lax.axis_size("gx")
    fits = (
        n_gx == 2
        and inputs.shape[0] == 2
        and inputs.shape[1] == 16
        and n_gy == KV
        and w_key.shape[1] == HD
        and cache_keys.shape[1] % 128 == 0
    )
    return on_device_kernel(*args) if fits else on_device_plain(*args)


def solution(mesh):
    return jax.shard_map(
        on_device,
        mesh=mesh,
        in_specs=(
            P(None, "ga", None),
            P(),
            P("gx", "gy"),
            P("gx", "gy"),
            P("gx", "gy"),
            P("gx", "gy"),
            P("ga", "gy", "gx"),
            P("ga", "gy", "gx"),
            P("ga"),
        ),
        out_specs=(P(None, "ga", ("gy", "gx")), P(None, "ga", None, "gx")),
        check_vma=False,
    )
```

```python
import functools
import math

import jax
import jax.numpy as jnp
import numpy as np
from jax import lax
from jax.experimental import pallas as pl
from jax.experimental.pallas import tpu as pltpu
from jax.sharding import PartitionSpec as P

HQ = 64
KV = 8
HD = 128


THETA = 500000.0
EPS = 1e-05


def rotate(values, positions):
    half_width = values.shape[-1] // 2
    frequency = jnp.exp(
        jnp.arange(half_width, dtype=jnp.float32) * (-2.0 * math.log(THETA) / values.shape[-1])
    )
    angles = positions[..., None, None] * frequency
    cos_part = jnp.cos(angles)
    sine_part = jnp.sin(angles)
    first_half = values[..., :half_width]
    second_half = values[..., half_width:]
    return jnp.concatenate(
        [
            first_half * cos_part - second_half * sine_part,
            second_half * cos_part + first_half * sine_part,
        ],
        axis=-1,
    )


def on_device_plain(
    inputs, norm_gain, w_query, w_key, w_value, output_weight, cache_keys, cache_values, lengths
):
    n_gx = lax.axis_size("gx")
    gx_pos = lax.axis_index("gx")
    gy_pos = lax.axis_index("gy")
    steps_total = inputs.shape[0]
    batch_rows = inputs.shape[1]
    input_half_width = w_query.shape[0]
    cache_span = cache_keys.shape[1]
    kv_local = cache_keys.shape[2]
    heads_kv = kv_local // HD
    group_size = HQ // KV
    heads_here = heads_kv * group_size
    q_width = heads_here * HD
    output_columns = output_weight.shape[1]
    own_cols = output_columns // n_gx
    score_scale = HD ** (-0.5)
    states = inputs.astype(jnp.float32)
    normalized_input = (
        states
        * lax.rsqrt(jnp.mean(states * states, axis=-1, keepdims=True) + EPS)
        * norm_gain.astype(jnp.float32)
    ).astype(jnp.bfloat16)
    block = lax.dynamic_slice_in_dim(
        normalized_input, gx_pos * input_half_width, input_half_width, 2
    )
    residual_cols = lax.dynamic_slice_in_dim(
        states, gy_pos * output_columns + gx_pos * own_cols, own_cols, 2
    )
    offsets = gy_pos * cache_span + jnp.arange(cache_span, dtype=jnp.int32)
    valid_mask = offsets[None, :] < lengths[:, None]
    keys_here = cache_keys.reshape(batch_rows, cache_span, heads_kv, HD)
    values_here = cache_values.reshape(batch_rows, cache_span, heads_kv, HD)
    q_part = jnp.einsum("cbd,de->cbe", block, w_query, preferred_element_type=jnp.float32)
    k_part = jnp.einsum("cbd,de->cbe", block, w_key, preferred_element_type=jnp.float32)
    v_part = jnp.einsum("cbd,de->cbe", block, w_value, preferred_element_type=jnp.float32)
    q_sum, k_sum, v_sum = lax.psum((q_part, k_part, v_part), "gx")
    positions = (
        lengths.astype(jnp.float32)[None, :]
        + jnp.arange(steps_total, dtype=jnp.float32)[:, None]
    )
    gather = lambda a: lax.all_gather(a, "gy", axis=2, tiled=True)
    mine = lambda a, width: lax.dynamic_slice_in_dim(a, gx_pos * width, width, 2)
    q_all = gather(
        q_sum.astype(jnp.float32)
        if q_sum.shape[2] % HD
        else rotate(q_sum.reshape(steps_total, batch_rows, -1, HD), positions)
        .astype(jnp.bfloat16)
        .reshape(q_sum.shape)
    )
    queries = mine(q_all, q_width).reshape(steps_total, batch_rows, heads_kv, group_size, HD)
    if q_sum.shape[2] % HD:
        queries = rotate(
            queries.reshape(steps_total, batch_rows, -1, HD), positions
        ).astype(jnp.bfloat16).reshape(queries.shape)
    keys_raw = mine(gather(k_sum.astype(jnp.bfloat16)), kv_local)
    values_new = mine(gather(v_sum.astype(jnp.bfloat16)), kv_local)
    keys_new = (
        rotate(keys_raw.astype(jnp.float32).reshape(steps_total, batch_rows, heads_kv, HD), positions)
        .astype(jnp.bfloat16)
        .reshape(steps_total, batch_rows, kv_local)
    )
    fresh_all = jnp.stack([keys_new, values_new], axis=2)
    cache_score = (
        jnp.einsum("cbkgd,bpkd->bkcgp", queries, keys_here, preferred_element_type=jnp.float32)
        * score_scale
    )
    cache_score = jnp.where(valid_mask[:, None, None, None, :], cache_score, -jnp.inf)
    fresh_score = (
        jnp.einsum(
            "cbkgd,jbkd->bkcgj",
            queries,
            keys_new.reshape(steps_total, batch_rows, heads_kv, HD),
            preferred_element_type=jnp.float32,
        )
        * score_scale
    )
    order = jnp.arange(steps_total, dtype=jnp.int32)
    causal = order[None, :] <= order[:, None]
    fresh_score = jnp.where(causal[:, None, :], fresh_score, -jnp.inf)
    local_peak = jnp.maximum(jnp.max(cache_score, axis=-1), jnp.max(fresh_score, axis=-1))
    peak_score = lax.pmax(local_peak, "gy")
    cache_weight = jnp.exp(cache_score - peak_score[..., None])
    fresh_weight = jnp.exp(fresh_score - peak_score[..., None])
    cache_total = jnp.sum(cache_weight, axis=-1)
    fresh_total = jnp.sum(fresh_weight, axis=-1)
    cache_acc = jnp.einsum(
        "bkcgp,bpkd->bkcgd",
        cache_weight.astype(jnp.bfloat16),
        values_here,
        preferred_element_type=jnp.float32,
    )
    fresh_acc = jnp.einsum(
        "bkcgj,jbkd->bkcgd",
        fresh_weight.astype(jnp.bfloat16),
        values_new.reshape(steps_total, batch_rows, heads_kv, HD),
        preferred_element_type=jnp.float32,
    )
    acc_sum, total_sum = lax.psum((cache_acc, cache_total), "gy")
    attention_result = ((acc_sum + fresh_acc) / (total_sum + fresh_total)[..., None]).astype(
        jnp.bfloat16
    )
    attention_result = jnp.transpose(attention_result, (2, 0, 1, 3, 4)).reshape(
        steps_total, batch_rows, q_width
    )
    output_piece = jnp.einsum(
        "yjz,zo->yjo", attention_result, output_weight, preferred_element_type=jnp.float32
    )
    projected = lax.psum_scatter(output_piece, "gx", scatter_dimension=2, tiled=True)
    mixed_all = (residual_cols + projected).astype(jnp.bfloat16)
    return (mixed_all, fresh_all)


MESH = pl.DeviceIdType.MESH
LOW = -1e30
CHUNKS = 8
VMEM_BYTES = 64 * 1024 * 1024


def block_kernel(
    n_gy,
    len_hbm, gain_ref, freq_hbm, x_hbm, wq_hbm, wk_hbm, wv_hbm, wo_hbm, kc_hbm, vc_hbm,
    mixed_ref, fresh_ref,
    len_ref, freq_ref,
    x_v, xn_v, w_v, wo_v, kc_v, vc_v, part, part_in, qsort, pack, gath, kvf,
    acc_s, acc_r, ml_s, ml_r, fresh_acc, att, flat, lhs, po_s, po_r,
    sem_len, sem_freq, sem_x, sem_wq, sem_wk, sem_wv, sem_kc, sem_vc, sem_wo,
    pair_s, pair_r, gath_s, gath_r, fwd_s, accs, accr, mls, mlr, atts, attr, out_s, out_r,
):
    gx = lax.axis_index("gx")
    gy = lax.axis_index("gy")
    half = w_v.shape[0]
    qw = wq_hbm.shape[1]
    heads = kc_hbm.shape[2] // HD
    rows = kc_hbm.shape[0]
    span = kc_hbm.shape[1]
    own = rows // n_gy
    group = HQ // KV
    hb = rows // 2
    combos = own * heads
    per_gx = n_gy // 2
    target = gy // per_gx
    scale = HD ** (-0.5)
    step_rows = half // CHUNKS

    def owner_of(d):
        return lax.rem(gy + 1 + d, n_gy)

    copy_x = pltpu.make_async_copy(x_hbm, x_v, sem_x)
    copy_x.start()
    copy_len = pltpu.make_async_copy(len_hbm, len_ref, sem_len)
    copy_len.start()
    copy_freq = pltpu.make_async_copy(freq_hbm, freq_ref, sem_freq)
    copy_freq.start()

    def wq_copies(c):
        r = pl.ds(c * step_rows, step_rows)
        return (
            pltpu.make_async_copy(wq_hbm.at[r], w_v.at[r, pl.ds(0, qw)], sem_wq.at[c]),
            pltpu.make_async_copy(wk_hbm.at[r], w_v.at[r, pl.ds(qw, HD)], sem_wk.at[c]),
            pltpu.make_async_copy(wv_hbm.at[r], w_v.at[r, pl.ds(qw + HD, HD)], sem_wv.at[c]),
        )

    def cache_copies(d):
        r = pl.ds(owner_of(d) * own, own)
        return (
            pltpu.make_async_copy(kc_hbm.at[r], kc_v.at[d], sem_kc.at[d]),
            pltpu.make_async_copy(vc_hbm.at[r], vc_v.at[d], sem_vc.at[d]),
        )

    oc = wo_hbm.shape[1] // 2
    ok = half // 4

    def wo_copy(p, c):
        which = (1 - gx) if p == 0 else gx
        r = pl.ds(c * ok, ok)
        return pltpu.make_async_copy(
            wo_hbm.at[r, pl.ds(pl.multiple_of(which * oc, oc), oc)], wo_v.at[p, r], sem_wo.at[p * 4 + c]
        )

    for c in range(CHUNKS):
        for copy in wq_copies(c):
            copy.start()

    barrier = pltpu.get_barrier_semaphore()
    for d in range(1, n_gy):
        for g in range(2):
            pl.semaphore_signal(
                barrier, inc=1, device_id={"gy": lax.rem(gy + d, n_gy), "gx": g}, device_id_type=MESH
            )
    pl.semaphore_signal(barrier, inc=1, device_id={"gx": 1 - gx}, device_id_type=MESH)

    copy_len.wait()
    copy_freq.wait()

    row16 = lax.broadcasted_iota(jnp.int32, (2 * hb, HD), 0)
    lane16 = lax.broadcasted_iota(jnp.int32, (2 * hb, HD), 1)
    pos = jnp.zeros((2 * hb, HD), jnp.float32)
    for r in range(hb):
        pos = jnp.where(row16 % hb == r, len_ref[gx * hb + r].astype(jnp.float32), pos)
    pos = pos + (row16 // hb).astype(jnp.float32)
    angle = pos * freq_ref[...]
    cos_t = jnp.cos(angle)
    sin_t = jnp.sin(angle)
    sin_t = jnp.where(lane16 < HD // 2, -sin_t, sin_t)

    def rope(u):
        return u * cos_t + pltpu.roll(u, HD // 2, 1) * sin_t

    copy_x.wait()
    width = x_v.shape[1]
    total = jnp.zeros((x_v.shape[0], 1024), jnp.float32)
    for c in range(width // 1024):
        xf = x_v[:, c * 1024 : (c + 1) * 1024].astype(jnp.float32)
        total = total + xf * xf
    inv = lax.rsqrt(jnp.sum(total, axis=1, keepdims=True) * (1.0 / width) + EPS)
    for c in range(half // 1024):
        cols = pl.ds(pl.multiple_of(gx * half + c * 1024, 1024), 1024)
        xf = x_v[:, cols].astype(jnp.float32)
        xn_v[:, c * 1024 : (c + 1) * 1024] = (xf * inv * gain_ref[:, cols]).astype(jnp.bfloat16)

    acc = jnp.zeros((x_v.shape[0], w_v.shape[1]), jnp.float32)
    for c in range(CHUNKS):
        for copy in wq_copies(c):
            copy.wait()
        if c >= CHUNKS - 4:
            for d in range(2 * (c - CHUNKS + 4), 2 * (c - CHUNKS + 5)):
                for copy in cache_copies(d):
                    copy.start()
        r = slice(c * step_rows, (c + 1) * step_rows)
        acc = acc + jnp.dot(xn_v[:, r], w_v[r, :], preferred_element_type=jnp.float32)
    for c in range(2):
        for s in range(2):
            part[c, s * hb : (s + 1) * hb, :] = acc[s * rows + c * hb : s * rows + (c + 1) * hb]

    pl.semaphore_wait(barrier, 2 * n_gy - 1)
    pair = pltpu.make_async_remote_copy(
        src_ref=part.at[1 - gx], dst_ref=part_in, send_sem=pair_s, recv_sem=pair_r,
        device_id={"gx": 1 - gx}, device_id_type=MESH,
    )
    pair.start()
    pair.wait_recv()
    for p in range(2):
        for c in range(4):
            wo_copy(p, c).start()
    tot = part[gx] + part_in[...]
    for g in range(group):
        u = rope(tot[:, g * HD : (g + 1) * HD])
        for s in range(2):
            qsort[pl.ds(s * group + g, hb, stride=2 * group), :] = u[s * hb : (s + 1) * hb]
    nq = hb * 2 * group
    pack[0:nq, :] = qsort[...].astype(jnp.bfloat16)
    kraw = tot[:, qw : qw + HD].astype(jnp.bfloat16).astype(jnp.float32)
    pack[nq : nq + 2 * hb, :] = rope(kraw).astype(jnp.bfloat16)
    pack[nq + 2 * hb : nq + 4 * hb, :] = tot[:, qw + HD : qw + 2 * HD].astype(jnp.bfloat16)

    slot = lax.rem(gy, per_gx) * 2 + gx
    here = target == gx

    def gather_copy(i, at):
        return pltpu.make_async_remote_copy(
            src_ref=pack, dst_ref=gath.at[at], send_sem=gath_s.at[i], recv_sem=gath_r.at[at],
            device_id={"gy": lax.rem(gy + 2 * i, n_gy), "gx": target}, device_id_type=MESH,
        )

    for i in range(1, n_gy // 2):
        gather_copy(i, slot).start()

    @pl.when(here)
    def _():
        gath[slot] = pack[...]

    @pl.when(jnp.logical_not(here))
    def _():
        gather_copy(0, slot).start()

    odd = lax.rem(gy, 2)
    across = gy + 1 - 2 * odd

    def forward(j):
        at = (j // 2) * 4 + odd * 2 + j % 2
        return at, pltpu.make_async_remote_copy(
            src_ref=gath.at[at], dst_ref=gath.at[at], send_sem=fwd_s.at[j], recv_sem=gath_r.at[at],
            device_id={"gy": across}, device_id_type=MESH,
        )

    for j in range(heads):
        at, onward = forward(j)
        mine = jnp.logical_and(here, slot == at)

        @pl.when(jnp.logical_not(mine))
        def _():
            gather_copy(1, at).wait_recv()

        onward.start()
    for j in range(heads):
        gather_copy(1, (j // 2) * 4 + (1 - odd) * 2 + j % 2).wait_recv()

    lane_ml = lax.broadcasted_iota(jnp.int32, (2 * group, HD), 1)
    lane_s = lax.broadcasted_iota(jnp.int32, (2 * group, span), 1) + gy * span

    def send_acc(d):
        return pltpu.make_async_remote_copy(
            src_ref=acc_s.at[d], dst_ref=acc_r.at[d], send_sem=accs.at[d], recv_sem=accr.at[d],
            device_id={"gy": owner_of(d)}, device_id_type=MESH,
        )

    def send_ml(d):
        return pltpu.make_async_remote_copy(
            src_ref=ml_s.at[d], dst_ref=ml_r.at[d], send_sem=mls.at[d], recv_sem=mlr.at[d],
            device_id={"gy": owner_of(d)}, device_id_type=MESH,
        )

    nqr = 2 * group

    def attend(d, carry):
        for copy in cache_copies(d):
            copy.wait()
        owner = owner_of(d)
        ml = jnp.zeros((nqr, HD), jnp.float32)
        ks = [(i, h) for i in range(own) for h in range(heads)]
        rows_b = [owner * own + i for i in range(own)]
        seen = [lane_s < len_ref[b] for b in rows_b]
        scores = [
            lax.dot_general(
                gath[h * 2 + rows_b[i] // hb,
                     pl.ds(pl.multiple_of(lax.rem(rows_b[i], hb) * nqr, nqr), nqr), :],
                kc_v[d, i, :, h * HD : (h + 1) * HD], (((1,), (1,)), ((), ())),
                preferred_element_type=jnp.float32,
            )
            for i, h in ks
        ]
        scores = [jnp.where(seen[i], s * scale, LOW) for (i, h), s in zip(ks, scores)]
        peaks = [jnp.max(s, axis=1, keepdims=True) for s in scores]
        probs = [jnp.where(seen[i], jnp.exp(s - m), 0.0) for (i, h), s, m in zip(ks, scores, peaks)]
        outs = [
            jnp.dot(
                p.astype(jnp.bfloat16), vc_v[d, i, :, h * HD : (h + 1) * HD],
                preferred_element_type=jnp.float32,
            )
            for (i, h), p in zip(ks, probs)
        ]
        sums = [jnp.sum(p, axis=1, keepdims=True) for p in probs]
        for k in range(combos):
            acc_s[d, k * nqr : (k + 1) * nqr, :] = outs[k].astype(jnp.bfloat16)
            ml = jnp.where(lane_ml == k, peaks[k], ml)
            ml = jnp.where(lane_ml == k + HD // 2, sums[k], ml)
        ml_s[d] = ml

        @pl.when(d < n_gy - 1)
        def _():
            send_acc(d).start()
            send_ml(d).start()

        return carry

    lax.fori_loop(0, n_gy, attend, 0)

    for k in range(2 * heads):
        kvf[k] = gath[k, nq : nq + 4 * hb, :].astype(jnp.float32)
    for s in range(2):
        for t in range(2):
            for h in range(heads):
                at = t * 2 * hb + s * hb
                fresh_ref[s * rows : (s + 1) * rows, (t * heads + h) * HD : (t * heads + h + 1) * HD] = (
                    jnp.concatenate([kvf[2 * h, at : at + hb, :], kvf[2 * h + 1, at : at + hb, :]], axis=0)
                ).astype(jnp.bfloat16)

    later = lax.broadcasted_iota(jnp.int32, (nqr, 1), 0) >= group
    mlf = jnp.zeros((nqr, HD), jnp.float32)
    for i in range(own):
        b = gy * own + i
        c = b // hb
        bl = lax.rem(b, hb)
        for h in range(heads):
            k = i * heads + h
            q = gath[h * 2 + c, pl.ds(pl.multiple_of(bl * nqr, nqr), nqr), :].astype(jnp.float32)
            f = []
            for s in range(2):
                key = kvf[h * 2 + c, pl.ds(s * hb + bl, 1), :]
                f.append(jnp.sum(q * key, axis=1, keepdims=True) * scale)
            f[1] = jnp.where(later, f[1], LOW)
            m = jnp.maximum(f[0], f[1])
            p0 = jnp.exp(f[0] - m)
            p1 = jnp.where(later, jnp.exp(f[1] - m), 0.0)
            v0 = kvf[h * 2 + c, pl.ds(2 * hb + bl, 1), :]
            v1 = kvf[h * 2 + c, pl.ds(3 * hb + bl, 1), :]
            fresh_acc[k * nqr : (k + 1) * nqr, :] = (
                p0.astype(jnp.bfloat16).astype(jnp.float32) * v0
                + p1.astype(jnp.bfloat16).astype(jnp.float32) * v1
            )
            mlf = jnp.where(lane_ml == k, m, mlf)
            mlf = jnp.where(lane_ml == k + HD // 2, p0 + p1, mlf)

    for d in range(n_gy - 1):
        send_ml(d).wait_recv()
    ml_all = [ml_r[d] for d in range(n_gy - 1)] + [ml_s[n_gy - 1], mlf]
    peak = ml_all[0]
    for ml in ml_all[1:]:
        peak = jnp.maximum(peak, ml)
    factors = [jnp.exp(ml - peak) for ml in ml_all]
    weight = jnp.zeros_like(peak)
    for f, ml in zip(factors, ml_all):
        weight = weight + f * pltpu.roll(ml, HD // 2, 1)
    for d in range(n_gy - 1):
        send_acc(d).wait_recv()
    for k in range(combos):
        r = slice(k * nqr, (k + 1) * nqr)
        o = factors[n_gy][:, k : k + 1] * fresh_acc[r, :]
        for d in range(n_gy):
            a = acc_r[d, r, :] if d < n_gy - 1 else acc_s[d, r, :]
            o = o + factors[d][:, k : k + 1] * a.astype(jnp.float32)
        att[gy, r, :] = (o / weight[:, k : k + 1]).astype(jnp.bfloat16)

    def att_copy(n, to, at):
        return pltpu.make_async_remote_copy(
            src_ref=att.at[at], dst_ref=att.at[at], send_sem=atts.at[n], recv_sem=attr.at[at],
            device_id={"gy": to}, device_id_type=MESH,
        )

    side = n_gy // 2
    sends = [att_copy(i - 1, lax.rem(gy + 2 * i, n_gy), gy) for i in range(1, side)]
    sends.append(att_copy(side - 1, across, gy))
    for copy in sends:
        copy.start()
    for i in range(1, side):
        at = lax.rem(gy + 2 * i, n_gy)
        onward = att_copy(side - 1 + i, across, at)
        onward.wait_recv()
        onward.start()
        sends.append(onward)
    for i in range(side):
        att_copy(0, across, lax.rem(across + 2 * i, n_gy)).wait_recv()
    size = combos * nqr
    for j in range(n_gy):
        flat[j * size : (j + 1) * size, :] = att[j].astype(jnp.float32)
    for h in range(heads):
        for g in range(group):
            for s in range(2):
                lhs[s * rows : (s + 1) * rows, (h * group + g) * HD : (h * group + g + 1) * HD] = flat[
                    pl.ds(h * nqr + s * group + g, rows, stride=heads * nqr), :
                ].astype(jnp.bfloat16)

    def project(p):
        total = jnp.zeros((2 * rows, oc), jnp.float32)
        for c in range(4):
            wo_copy(p, c).wait()
            r = slice(c * ok, (c + 1) * ok)
            total = total + jnp.dot(lhs[:, r], wo_v[p, r, :], preferred_element_type=jnp.float32)
        return total

    po_s[...] = project(0)
    out_copy = pltpu.make_async_remote_copy(
        src_ref=po_s, dst_ref=po_r, send_sem=out_s, recv_sem=out_r,
        device_id={"gx": 1 - gx}, device_id_type=MESH,
    )
    out_copy.start()
    mine_out = project(1)
    residual = x_v[:, pl.ds(pl.multiple_of((gy * 2 + gx) * oc, oc), oc)].astype(jnp.float32)
    out_copy.wait_recv()
    mixed_ref[...] = (residual + (mine_out + po_r[...])).astype(jnp.bfloat16)

    pair.wait_send()
    for i in range(1, n_gy // 2):
        gather_copy(i, slot).wait_send()
    for j in range(heads):
        forward(j)[1].wait_send()

    @pl.when(jnp.logical_not(here))
    def _():
        gather_copy(0, slot).wait_send()

    for d in range(n_gy - 1):
        send_acc(d).wait_send()
        send_ml(d).wait_send()
    for copy in sends:
        copy.wait_send()
    out_copy.wait_send()


def on_device_kernel(
    inputs, norm_gain, w_query, w_key, w_value, output_weight, cache_keys, cache_values, lengths
):
    n_gy = lax.axis_size("gy")
    steps, rows, width = inputs.shape
    half, qw = w_query.shape
    span, kvl = cache_keys.shape[1:]
    heads = kvl // HD
    own = rows // n_gy
    group = HQ // KV
    nqr = 2 * group
    hb = rows // 2
    size = own * heads * nqr
    oc = output_weight.shape[1] // 2
    npack = hb * nqr + 4 * hb
    freq = np.exp(np.arange(HD // 2) * (-2.0 * math.log(THETA) / HD))
    freq = jnp.asarray(np.tile(freq, 2)[None, :], jnp.float32)
    f32, b16 = jnp.float32, jnp.bfloat16
    dma = pltpu.SemaphoreType.DMA
    vmem = pl.BlockSpec(memory_space=pltpu.VMEM)
    hbm = pl.BlockSpec(memory_space=pltpu.HBM)
    mixed, fresh = pl.pallas_call(
        functools.partial(block_kernel, n_gy),
        out_shape=(
            jax.ShapeDtypeStruct((steps * rows, oc), b16),
            jax.ShapeDtypeStruct((steps * rows, 2 * kvl), b16),
        ),
        in_specs=[hbm, vmem] + [hbm] * 8,
        out_specs=(vmem, vmem),
        scratch_shapes=[
            pltpu.SMEM((rows,), jnp.int32),
            pltpu.VMEM((1, HD), f32),
            pltpu.VMEM((steps * rows, width), b16),
            pltpu.VMEM((steps * rows, half), b16),
            pltpu.VMEM((half, qw + 2 * HD), b16),
            pltpu.VMEM((2, half, oc), b16),
            pltpu.VMEM((n_gy, own, span, kvl), b16),
            pltpu.VMEM((n_gy, own, span, kvl), b16),
            pltpu.VMEM((2, steps * hb, qw + 2 * HD), f32),
            pltpu.VMEM((steps * hb, qw + 2 * HD), f32),
            pltpu.VMEM((hb * nqr, HD), f32),
            pltpu.VMEM((npack, HD), b16),
            pltpu.VMEM((2 * heads, npack, HD), b16),
            pltpu.VMEM((2 * heads, 4 * hb, HD), f32),
            pltpu.VMEM((n_gy, size, HD), b16),
            pltpu.VMEM((n_gy - 1, size, HD), b16),
            pltpu.VMEM((n_gy, nqr, HD), f32),
            pltpu.VMEM((n_gy - 1, nqr, HD), f32),
            pltpu.VMEM((size, HD), f32),
            pltpu.VMEM((n_gy, size, HD), b16),
            pltpu.VMEM((n_gy * size, HD), f32),
            pltpu.VMEM((steps * rows, half), b16),
            pltpu.VMEM((steps * rows, oc), f32),
            pltpu.VMEM((steps * rows, oc), f32),
            dma, dma, dma, dma((CHUNKS,)), dma((CHUNKS,)), dma((CHUNKS,)), dma((n_gy,)), dma((n_gy,)), dma((8,)),
            dma, dma, dma((n_gy // 2,)), dma((2 * heads,)), dma((heads,)),
            dma((n_gy - 1,)), dma((n_gy - 1,)), dma((n_gy - 1,)), dma((n_gy - 1,)),
            dma((n_gy - 1,)), dma((n_gy,)), dma, dma,
        ],
        compiler_params=pltpu.CompilerParams(
            collective_id=0, has_side_effects=True, vmem_limit_bytes=VMEM_BYTES
        ),
        name="decode_block",
    )(
        lengths, norm_gain.astype(f32).reshape(1, width), freq, inputs.reshape(steps * rows, width),
        w_query, w_key, w_value, output_weight, cache_keys, cache_values,
    )
    return mixed.reshape(steps, rows, oc), fresh.reshape(steps, rows, 2, kvl)


def on_device(*args):
    inputs, _, w_query, w_key, _, output_weight, cache_keys, _, _ = args
    n_gy, n_gx = lax.axis_size("gy"), lax.axis_size("gx")
    fits = (
        n_gx == 2
        and inputs.shape[0] == 2
        and inputs.shape[1] == 16
        and n_gy == KV
        and w_key.shape[1] == HD
        and cache_keys.shape[1] % 128 == 0
    )
    return on_device_kernel(*args) if fits else on_device_plain(*args)


def solution(mesh):
    return jax.shard_map(
        on_device,
        mesh=mesh,
        in_specs=(
            P(None, "ga", None),
            P(),
            P("gx", "gy"),
            P("gx", "gy"),
            P("gx", "gy"),
            P("gx", "gy"),
            P("ga", "gy", "gx"),
            P("ga", "gy", "gx"),
            P("ga"),
        ),
        out_specs=(P(None, "ga", ("gy", "gx")), P(None, "ga", None, "gx")),
        check_vma=False,
    )
```

```python
import functools
import math

import jax
import jax.numpy as jnp
import numpy as np
from jax import lax
from jax.experimental import pallas as pl
from jax.experimental.pallas import tpu as pltpu
from jax.sharding import PartitionSpec as P

HQ = 64
KV = 8
HD = 128


THETA = 500000.0
EPS = 1e-05


def rotate(values, positions):
    half_width = values.shape[-1] // 2
    frequency = jnp.exp(
        jnp.arange(half_width, dtype=jnp.float32) * (-2.0 * math.log(THETA) / values.shape[-1])
    )
    angles = positions[..., None, None] * frequency
    cos_part = jnp.cos(angles)
    sine_part = jnp.sin(angles)
    first_half = values[..., :half_width]
    second_half = values[..., half_width:]
    return jnp.concatenate(
        [
            first_half * cos_part - second_half * sine_part,
            second_half * cos_part + first_half * sine_part,
        ],
        axis=-1,
    )


def on_device_plain(
    inputs, norm_gain, w_query, w_key, w_value, output_weight, cache_keys, cache_values, lengths
):
    n_gx = lax.axis_size("gx")
    gx_pos = lax.axis_index("gx")
    gy_pos = lax.axis_index("gy")
    steps_total = inputs.shape[0]
    batch_rows = inputs.shape[1]
    input_half_width = w_query.shape[0]
    cache_span = cache_keys.shape[1]
    kv_local = cache_keys.shape[2]
    heads_kv = kv_local // HD
    group_size = HQ // KV
    heads_here = heads_kv * group_size
    q_width = heads_here * HD
    output_columns = output_weight.shape[1]
    own_cols = output_columns // n_gx
    score_scale = HD ** (-0.5)
    states = inputs.astype(jnp.float32)
    normalized_input = (
        states
        * lax.rsqrt(jnp.mean(states * states, axis=-1, keepdims=True) + EPS)
        * norm_gain.astype(jnp.float32)
    ).astype(jnp.bfloat16)
    block = lax.dynamic_slice_in_dim(
        normalized_input, gx_pos * input_half_width, input_half_width, 2
    )
    residual_cols = lax.dynamic_slice_in_dim(
        states, gy_pos * output_columns + gx_pos * own_cols, own_cols, 2
    )
    offsets = gy_pos * cache_span + jnp.arange(cache_span, dtype=jnp.int32)
    valid_mask = offsets[None, :] < lengths[:, None]
    keys_here = cache_keys.reshape(batch_rows, cache_span, heads_kv, HD)
    values_here = cache_values.reshape(batch_rows, cache_span, heads_kv, HD)
    q_part = jnp.einsum("cbd,de->cbe", block, w_query, preferred_element_type=jnp.float32)
    k_part = jnp.einsum("cbd,de->cbe", block, w_key, preferred_element_type=jnp.float32)
    v_part = jnp.einsum("cbd,de->cbe", block, w_value, preferred_element_type=jnp.float32)
    q_sum, k_sum, v_sum = lax.psum((q_part, k_part, v_part), "gx")
    positions = (
        lengths.astype(jnp.float32)[None, :]
        + jnp.arange(steps_total, dtype=jnp.float32)[:, None]
    )
    gather = lambda a: lax.all_gather(a, "gy", axis=2, tiled=True)
    mine = lambda a, width: lax.dynamic_slice_in_dim(a, gx_pos * width, width, 2)
    q_all = gather(
        q_sum.astype(jnp.float32)
        if q_sum.shape[2] % HD
        else rotate(q_sum.reshape(steps_total, batch_rows, -1, HD), positions)
        .astype(jnp.bfloat16)
        .reshape(q_sum.shape)
    )
    queries = mine(q_all, q_width).reshape(steps_total, batch_rows, heads_kv, group_size, HD)
    if q_sum.shape[2] % HD:
        queries = rotate(
            queries.reshape(steps_total, batch_rows, -1, HD), positions
        ).astype(jnp.bfloat16).reshape(queries.shape)
    keys_raw = mine(gather(k_sum.astype(jnp.bfloat16)), kv_local)
    values_new = mine(gather(v_sum.astype(jnp.bfloat16)), kv_local)
    keys_new = (
        rotate(keys_raw.astype(jnp.float32).reshape(steps_total, batch_rows, heads_kv, HD), positions)
        .astype(jnp.bfloat16)
        .reshape(steps_total, batch_rows, kv_local)
    )
    fresh_all = jnp.stack([keys_new, values_new], axis=2)
    cache_score = (
        jnp.einsum("cbkgd,bpkd->bkcgp", queries, keys_here, preferred_element_type=jnp.float32)
        * score_scale
    )
    cache_score = jnp.where(valid_mask[:, None, None, None, :], cache_score, -jnp.inf)
    fresh_score = (
        jnp.einsum(
            "cbkgd,jbkd->bkcgj",
            queries,
            keys_new.reshape(steps_total, batch_rows, heads_kv, HD),
            preferred_element_type=jnp.float32,
        )
        * score_scale
    )
    order = jnp.arange(steps_total, dtype=jnp.int32)
    causal = order[None, :] <= order[:, None]
    fresh_score = jnp.where(causal[:, None, :], fresh_score, -jnp.inf)
    local_peak = jnp.maximum(jnp.max(cache_score, axis=-1), jnp.max(fresh_score, axis=-1))
    peak_score = lax.pmax(local_peak, "gy")
    cache_weight = jnp.exp(cache_score - peak_score[..., None])
    fresh_weight = jnp.exp(fresh_score - peak_score[..., None])
    cache_total = jnp.sum(cache_weight, axis=-1)
    fresh_total = jnp.sum(fresh_weight, axis=-1)
    cache_acc = jnp.einsum(
        "bkcgp,bpkd->bkcgd",
        cache_weight.astype(jnp.bfloat16),
        values_here,
        preferred_element_type=jnp.float32,
    )
    fresh_acc = jnp.einsum(
        "bkcgj,jbkd->bkcgd",
        fresh_weight.astype(jnp.bfloat16),
        values_new.reshape(steps_total, batch_rows, heads_kv, HD),
        preferred_element_type=jnp.float32,
    )
    acc_sum, total_sum = lax.psum((cache_acc, cache_total), "gy")
    attention_result = ((acc_sum + fresh_acc) / (total_sum + fresh_total)[..., None]).astype(
        jnp.bfloat16
    )
    attention_result = jnp.transpose(attention_result, (2, 0, 1, 3, 4)).reshape(
        steps_total, batch_rows, q_width
    )
    output_piece = jnp.einsum(
        "yjz,zo->yjo", attention_result, output_weight, preferred_element_type=jnp.float32
    )
    projected = lax.psum_scatter(output_piece, "gx", scatter_dimension=2, tiled=True)
    mixed_all = (residual_cols + projected).astype(jnp.bfloat16)
    return (mixed_all, fresh_all)


MESH = pl.DeviceIdType.MESH
LOW = -1e30
CHUNKS = 8
VMEM_BYTES = (64 * 1024 - 320) * 1024


def block_kernel(
    n_gy,
    len_hbm, gain_ref, freq_hbm, x_hbm, wq_hbm, wk_hbm, wv_hbm, wo_hbm, kc_hbm, vc_hbm,
    mixed_ref, fresh_ref,
    len_ref, freq_ref,
    x_v, xn_v, w_v, wo_v, kc_v, vc_v, part, part_in, qsort, pack, gath, kvf,
    acc_s, acc_r, ml_s, ml_r, fresh_acc, att, flat, lhs, po_s, po_r,
    sem_len, sem_freq, sem_x, sem_wq, sem_wk, sem_wv, sem_kc, sem_vc, sem_wo,
    pair_s, pair_r, gath_s, gath_r, accs, accr, mls, mlr, atts, attr, out_s, out_r,
):
    gx = lax.axis_index("gx")
    gy = lax.axis_index("gy")
    half = w_v.shape[0]
    qw = wq_hbm.shape[1]
    heads = kc_hbm.shape[2] // HD
    rows = kc_hbm.shape[0]
    span = kc_hbm.shape[1]
    own = rows // n_gy
    group = HQ // KV
    hb = rows // 2
    combos = own * heads
    per_gx = n_gy // 2
    target = gy // per_gx
    scale = HD ** (-0.5)
    step_rows = half // CHUNKS

    def owner_of(d):
        return lax.rem(gy + 1 + d, n_gy)

    copy_x = pltpu.make_async_copy(x_hbm, x_v, sem_x)
    copy_x.start()
    copy_len = pltpu.make_async_copy(len_hbm, len_ref, sem_len)
    copy_len.start()
    copy_freq = pltpu.make_async_copy(freq_hbm, freq_ref, sem_freq)
    copy_freq.start()

    def wq_copies(c):
        r = pl.ds(c * step_rows, step_rows)
        return (
            pltpu.make_async_copy(wq_hbm.at[r], w_v.at[r, pl.ds(0, qw)], sem_wq.at[c]),
            pltpu.make_async_copy(wk_hbm.at[r], w_v.at[r, pl.ds(qw, HD)], sem_wk.at[c]),
            pltpu.make_async_copy(wv_hbm.at[r], w_v.at[r, pl.ds(qw + HD, HD)], sem_wv.at[c]),
        )

    def cache_copies(d):
        r = pl.ds(owner_of(d) * own, own)
        return (
            pltpu.make_async_copy(kc_hbm.at[r], kc_v.at[d], sem_kc.at[d]),
            pltpu.make_async_copy(vc_hbm.at[r], vc_v.at[d], sem_vc.at[d]),
        )

    oc = wo_hbm.shape[1] // 2
    ok = half // 4

    def wo_copy(p, c):
        which = (1 - gx) if p == 0 else gx
        r = pl.ds(c * ok, ok)
        return pltpu.make_async_copy(
            wo_hbm.at[r, pl.ds(pl.multiple_of(which * oc, oc), oc)], wo_v.at[p, r], sem_wo.at[p * 4 + c]
        )

    for c in range(CHUNKS):
        for copy in wq_copies(c):
            copy.start()

    barrier = pltpu.get_barrier_semaphore()
    for d in range(1, n_gy):
        for g in range(2):
            pl.semaphore_signal(
                barrier, inc=1, device_id={"gy": lax.rem(gy + d, n_gy), "gx": g}, device_id_type=MESH
            )
    pl.semaphore_signal(barrier, inc=1, device_id={"gx": 1 - gx}, device_id_type=MESH)

    for d in range(n_gy):
        for copy in cache_copies(d):
            copy.start()
    for p in range(2):
        for c in range(4):
            wo_copy(p, c).start()

    copy_len.wait()
    copy_freq.wait()

    row16 = lax.broadcasted_iota(jnp.int32, (2 * hb, HD), 0)
    lane16 = lax.broadcasted_iota(jnp.int32, (2 * hb, HD), 1)
    pos = jnp.zeros((2 * hb, HD), jnp.float32)
    for r in range(hb):
        pos = jnp.where(row16 % hb == r, len_ref[gx * hb + r].astype(jnp.float32), pos)
    pos = pos + (row16 // hb).astype(jnp.float32)
    angle = pos * freq_ref[...]
    cos_t = jnp.cos(angle)
    sin_t = jnp.sin(angle)
    sin_t = jnp.where(lane16 < HD // 2, -sin_t, sin_t)

    def rope(u):
        return u * cos_t + pltpu.roll(u, HD // 2, 1) * sin_t

    copy_x.wait()
    width = x_v.shape[1]
    total = jnp.zeros((x_v.shape[0], 1024), jnp.float32)
    for c in range(width // 1024):
        xf = x_v[:, c * 1024 : (c + 1) * 1024].astype(jnp.float32)
        total = total + xf * xf
    inv = lax.rsqrt(jnp.sum(total, axis=1, keepdims=True) * (1.0 / width) + EPS)
    for c in range(half // 1024):
        cols = pl.ds(pl.multiple_of(gx * half + c * 1024, 1024), 1024)
        xf = x_v[:, cols].astype(jnp.float32)
        xn_v[:, c * 1024 : (c + 1) * 1024] = (xf * inv * gain_ref[:, cols]).astype(jnp.bfloat16)

    acc = jnp.zeros((x_v.shape[0], w_v.shape[1]), jnp.float32)
    for c in range(CHUNKS):
        for copy in wq_copies(c):
            copy.wait()
        r = slice(c * step_rows, (c + 1) * step_rows)
        acc = acc + jnp.dot(xn_v[:, r], w_v[r, :], preferred_element_type=jnp.float32)
    for c in range(2):
        for s in range(2):
            part[c, s * hb : (s + 1) * hb, :] = acc[s * rows + c * hb : s * rows + (c + 1) * hb]

    pl.semaphore_wait(barrier, 2 * n_gy - 1)
    pair = pltpu.make_async_remote_copy(
        src_ref=part.at[1 - gx], dst_ref=part_in, send_sem=pair_s, recv_sem=pair_r,
        device_id={"gx": 1 - gx}, device_id_type=MESH,
    )
    pair.start()
    pair.wait_recv()
    tot = part[gx] + part_in[...]
    for g in range(group):
        u = rope(tot[:, g * HD : (g + 1) * HD])
        for s in range(2):
            qsort[pl.ds(s * group + g, hb, stride=2 * group), :] = u[s * hb : (s + 1) * hb]
    nq = hb * 2 * group
    pack[0:nq, :] = qsort[...].astype(jnp.bfloat16)
    kraw = tot[:, qw : qw + HD].astype(jnp.bfloat16).astype(jnp.float32)
    pack[nq : nq + 2 * hb, :] = rope(kraw).astype(jnp.bfloat16)
    pack[nq + 2 * hb : nq + 4 * hb, :] = tot[:, qw + HD : qw + 2 * HD].astype(jnp.bfloat16)

    slot = lax.rem(gy, per_gx) * 2 + gx
    here = target == gx

    def gather_copy(i, at):
        return pltpu.make_async_remote_copy(
            src_ref=pack, dst_ref=gath.at[at], send_sem=gath_s.at[i], recv_sem=gath_r.at[at],
            device_id={"gy": lax.rem(gy + i, n_gy), "gx": target}, device_id_type=MESH,
        )

    for i in range(1, n_gy):
        gather_copy(i, slot).start()

    @pl.when(here)
    def _():
        gath[slot] = pack[...]

    @pl.when(jnp.logical_not(here))
    def _():
        gather_copy(0, slot).start()

    for k in range(2 * per_gx):
        mine = jnp.logical_and(here, slot == k)

        @pl.when(jnp.logical_not(mine))
        def _():
            gather_copy(1, k).wait_recv()

    lane_ml = lax.broadcasted_iota(jnp.int32, (2 * group, HD), 1)
    lane_s = lax.broadcasted_iota(jnp.int32, (2 * group, span), 1) + gy * span

    def send_acc(d):
        return pltpu.make_async_remote_copy(
            src_ref=acc_s.at[d], dst_ref=acc_r.at[d], send_sem=accs.at[d], recv_sem=accr.at[d],
            device_id={"gy": owner_of(d)}, device_id_type=MESH,
        )

    def send_ml(d):
        return pltpu.make_async_remote_copy(
            src_ref=ml_s.at[d], dst_ref=ml_r.at[d], send_sem=mls.at[d], recv_sem=mlr.at[d],
            device_id={"gy": owner_of(d)}, device_id_type=MESH,
        )

    nqr = 2 * group

    def attend(d, carry):
        for copy in cache_copies(d):
            copy.wait()
        owner = owner_of(d)
        ml = jnp.zeros((nqr, HD), jnp.float32)
        ks = [(i, h) for i in range(own) for h in range(heads)]
        rows_b = [owner * own + i for i in range(own)]
        seen = [lane_s < len_ref[b] for b in rows_b]
        scores = [
            lax.dot_general(
                gath[h * 2 + rows_b[i] // hb,
                     pl.ds(pl.multiple_of(lax.rem(rows_b[i], hb) * nqr, nqr), nqr), :],
                kc_v[d, i, :, h * HD : (h + 1) * HD], (((1,), (1,)), ((), ())),
                preferred_element_type=jnp.float32,
            )
            for i, h in ks
        ]
        scores = [jnp.where(seen[i], s * scale, LOW) for (i, h), s in zip(ks, scores)]
        peaks = [jnp.max(s, axis=1, keepdims=True) for s in scores]
        probs = [jnp.where(seen[i], jnp.exp(s - m), 0.0) for (i, h), s, m in zip(ks, scores, peaks)]
        outs = [
            jnp.dot(
                p.astype(jnp.bfloat16), vc_v[d, i, :, h * HD : (h + 1) * HD],
                preferred_element_type=jnp.float32,
            )
            for (i, h), p in zip(ks, probs)
        ]
        sums = [jnp.sum(p, axis=1, keepdims=True) for p in probs]
        for k in range(combos):
            acc_s[d, k * nqr : (k + 1) * nqr, :] = outs[k].astype(jnp.bfloat16)
            ml = jnp.where(lane_ml == k, peaks[k], ml)
            ml = jnp.where(lane_ml == k + HD // 2, sums[k], ml)
        ml_s[d] = ml

        @pl.when(d < n_gy - 1)
        def _():
            send_acc(d).start()
            send_ml(d).start()

        return carry

    lax.fori_loop(0, n_gy, attend, 0)

    for k in range(2 * heads):
        kvf[k] = gath[k, nq : nq + 4 * hb, :].astype(jnp.float32)
    for s in range(2):
        for t in range(2):
            for h in range(heads):
                at = t * 2 * hb + s * hb
                fresh_ref[s * rows : (s + 1) * rows, (t * heads + h) * HD : (t * heads + h + 1) * HD] = (
                    jnp.concatenate([kvf[2 * h, at : at + hb, :], kvf[2 * h + 1, at : at + hb, :]], axis=0)
                ).astype(jnp.bfloat16)

    later = lax.broadcasted_iota(jnp.int32, (nqr, 1), 0) >= group
    mlf = jnp.zeros((nqr, HD), jnp.float32)
    for i in range(own):
        b = gy * own + i
        c = b // hb
        bl = lax.rem(b, hb)
        for h in range(heads):
            k = i * heads + h
            q = gath[h * 2 + c, pl.ds(pl.multiple_of(bl * nqr, nqr), nqr), :].astype(jnp.float32)
            f = []
            for s in range(2):
                key = kvf[h * 2 + c, pl.ds(s * hb + bl, 1), :]
                f.append(jnp.sum(q * key, axis=1, keepdims=True) * scale)
            f[1] = jnp.where(later, f[1], LOW)
            m = jnp.maximum(f[0], f[1])
            p0 = jnp.exp(f[0] - m)
            p1 = jnp.where(later, jnp.exp(f[1] - m), 0.0)
            v0 = kvf[h * 2 + c, pl.ds(2 * hb + bl, 1), :]
            v1 = kvf[h * 2 + c, pl.ds(3 * hb + bl, 1), :]
            fresh_acc[k * nqr : (k + 1) * nqr, :] = (
                p0.astype(jnp.bfloat16).astype(jnp.float32) * v0
                + p1.astype(jnp.bfloat16).astype(jnp.float32) * v1
            )
            mlf = jnp.where(lane_ml == k, m, mlf)
            mlf = jnp.where(lane_ml == k + HD // 2, p0 + p1, mlf)

    for d in range(n_gy - 1):
        send_ml(d).wait_recv()
    ml_all = [ml_r[d] for d in range(n_gy - 1)] + [ml_s[n_gy - 1], mlf]
    peak = ml_all[0]
    for ml in ml_all[1:]:
        peak = jnp.maximum(peak, ml)
    factors = [jnp.exp(ml - peak) for ml in ml_all]
    weight = jnp.zeros_like(peak)
    for f, ml in zip(factors, ml_all):
        weight = weight + f * pltpu.roll(ml, HD // 2, 1)
    for d in range(n_gy - 1):
        send_acc(d).wait_recv()
    for k in range(combos):
        r = slice(k * nqr, (k + 1) * nqr)
        o = factors[n_gy][:, k : k + 1] * fresh_acc[r, :]
        for d in range(n_gy):
            a = acc_r[d, r, :] if d < n_gy - 1 else acc_s[d, r, :]
            o = o + factors[d][:, k : k + 1] * a.astype(jnp.float32)
        att[gy, r, :] = (o / weight[:, k : k + 1]).astype(jnp.bfloat16)

    def att_copy(d, at):
        return pltpu.make_async_remote_copy(
            src_ref=att.at[at], dst_ref=att.at[at], send_sem=atts.at[d - 1], recv_sem=attr.at[at],
            device_id={"gy": lax.rem(gy + d, n_gy)}, device_id_type=MESH,
        )

    for d in range(1, n_gy):
        att_copy(d, gy).start()
    for d in range(1, n_gy):
        att_copy(d, lax.rem(gy + d, n_gy)).wait_recv()
    size = combos * nqr
    for j in range(n_gy):
        flat[j * size : (j + 1) * size, :] = att[j].astype(jnp.float32)
    for h in range(heads):
        for g in range(group):
            for s in range(2):
                lhs[s * rows : (s + 1) * rows, (h * group + g) * HD : (h * group + g + 1) * HD] = flat[
                    pl.ds(h * nqr + s * group + g, rows, stride=heads * nqr), :
                ].astype(jnp.bfloat16)

    def project(p):
        total = jnp.zeros((2 * rows, oc), jnp.float32)
        for c in range(4):
            wo_copy(p, c).wait()
            r = slice(c * ok, (c + 1) * ok)
            total = total + jnp.dot(lhs[:, r], wo_v[p, r, :], preferred_element_type=jnp.float32)
        return total

    po_s[...] = project(0)
    out_copy = pltpu.make_async_remote_copy(
        src_ref=po_s, dst_ref=po_r, send_sem=out_s, recv_sem=out_r,
        device_id={"gx": 1 - gx}, device_id_type=MESH,
    )
    out_copy.start()
    mine_out = project(1)
    residual = x_v[:, pl.ds(pl.multiple_of((gy * 2 + gx) * oc, oc), oc)].astype(jnp.float32)
    out_copy.wait_recv()
    mixed_ref[...] = (residual + (mine_out + po_r[...])).astype(jnp.bfloat16)

    pair.wait_send()
    for i in range(1, n_gy):
        gather_copy(i, slot).wait_send()

    @pl.when(jnp.logical_not(here))
    def _():
        gather_copy(0, slot).wait_send()

    for d in range(n_gy - 1):
        send_acc(d).wait_send()
        send_ml(d).wait_send()
    for d in range(1, n_gy):
        att_copy(d, gy).wait_send()
    out_copy.wait_send()


def on_device_kernel(
    inputs, norm_gain, w_query, w_key, w_value, output_weight, cache_keys, cache_values, lengths
):
    n_gy = lax.axis_size("gy")
    steps, rows, width = inputs.shape
    half, qw = w_query.shape
    span, kvl = cache_keys.shape[1:]
    heads = kvl // HD
    own = rows // n_gy
    group = HQ // KV
    nqr = 2 * group
    hb = rows // 2
    size = own * heads * nqr
    oc = output_weight.shape[1] // 2
    npack = hb * nqr + 4 * hb
    freq = np.exp(np.arange(HD // 2) * (-2.0 * math.log(THETA) / HD))
    freq = jnp.asarray(np.tile(freq, 2)[None, :], jnp.float32)
    f32, b16 = jnp.float32, jnp.bfloat16
    dma = pltpu.SemaphoreType.DMA
    vmem = pl.BlockSpec(memory_space=pltpu.VMEM)
    hbm = pl.BlockSpec(memory_space=pltpu.HBM)
    mixed, fresh = pl.pallas_call(
        functools.partial(block_kernel, n_gy),
        out_shape=(
            jax.ShapeDtypeStruct((steps * rows, oc), b16),
            jax.ShapeDtypeStruct((steps * rows, 2 * kvl), b16),
        ),
        in_specs=[hbm, vmem] + [hbm] * 8,
        out_specs=(vmem, vmem),
        scratch_shapes=[
            pltpu.SMEM((rows,), jnp.int32),
            pltpu.VMEM((1, HD), f32),
            pltpu.VMEM((steps * rows, width), b16),
            pltpu.VMEM((steps * rows, half), b16),
            pltpu.VMEM((half, qw + 2 * HD), b16),
            pltpu.VMEM((2, half, oc), b16),
            pltpu.VMEM((n_gy, own, span, kvl), b16),
            pltpu.VMEM((n_gy, own, span, kvl), b16),
            pltpu.VMEM((2, steps * hb, qw + 2 * HD), f32),
            pltpu.VMEM((steps * hb, qw + 2 * HD), f32),
            pltpu.VMEM((hb * nqr, HD), f32),
            pltpu.VMEM((npack, HD), b16),
            pltpu.VMEM((2 * heads, npack, HD), b16),
            pltpu.VMEM((2 * heads, 4 * hb, HD), f32),
            pltpu.VMEM((n_gy, size, HD), b16),
            pltpu.VMEM((n_gy - 1, size, HD), b16),
            pltpu.VMEM((n_gy, nqr, HD), f32),
            pltpu.VMEM((n_gy - 1, nqr, HD), f32),
            pltpu.VMEM((size, HD), f32),
            pltpu.VMEM((n_gy, size, HD), b16),
            pltpu.VMEM((n_gy * size, HD), f32),
            pltpu.VMEM((steps * rows, half), b16),
            pltpu.VMEM((steps * rows, oc), f32),
            pltpu.VMEM((steps * rows, oc), f32),
            dma, dma, dma, dma((CHUNKS,)), dma((CHUNKS,)), dma((CHUNKS,)), dma((n_gy,)), dma((n_gy,)), dma((8,)),
            dma, dma, dma((n_gy,)), dma((2 * heads,)),
            dma((n_gy - 1,)), dma((n_gy - 1,)), dma((n_gy - 1,)), dma((n_gy - 1,)),
            dma((n_gy - 1,)), dma((n_gy,)), dma, dma,
        ],
        compiler_params=pltpu.CompilerParams(
            collective_id=0, has_side_effects=True, vmem_limit_bytes=VMEM_BYTES
        ),
        name="decode_block",
    )(
        lengths, norm_gain.astype(f32).reshape(1, width), freq, inputs.reshape(steps * rows, width),
        w_query, w_key, w_value, output_weight, cache_keys, cache_values,
    )
    return mixed.reshape(steps, rows, oc), fresh.reshape(steps, rows, 2, kvl)


def on_device(*args):
    inputs, _, w_query, w_key, _, output_weight, cache_keys, _, _ = args
    n_gy, n_gx = lax.axis_size("gy"), lax.axis_size("gx")
    fits = (
        n_gx == 2
        and inputs.shape[0] == 2
        and inputs.shape[1] == 16
        and n_gy == KV
        and w_key.shape[1] == HD
        and cache_keys.shape[1] % 128 == 0
    )
    return on_device_kernel(*args) if fits else on_device_plain(*args)


def solution(mesh):
    return jax.shard_map(
        on_device,
        mesh=mesh,
        in_specs=(
            P(None, "ga", None),
            P(),
            P("gx", "gy"),
            P("gx", "gy"),
            P("gx", "gy"),
            P("gx", "gy"),
            P("ga", "gy", "gx"),
            P("ga", "gy", "gx"),
            P("ga"),
        ),
        out_specs=(P(None, "ga", ("gy", "gx")), P(None, "ga", None, "gx")),
        check_vma=False,
    )
```
